256 devices in a mesh: row: 16 (over z, core), col: 16 (over y, x).
Axes of the slice: x: 4, y: 4, z: 8, core: 2. Of those that a mesh axis runs over, the one named last changes fastest.
Arguments:
- activations: bfloat16 [512, 8192], P('row', 'col'), may hold values from -6 to 6
- out_grads: bfloat16 [512, 29568], P('col', 'row'), may hold values from -6 to 6
- basis_in: bfloat16 [8192, 8192], P('col', 'row'), may hold values from -0.0625 to 0.0625
- basis_out: bfloat16 [29568, 29568], P('row', 'col'), may hold values from -0.03125 to 0.03125
- seq_lengths: int32 [8], replicated, may hold values from 1 to 256, 512 in all
Outputs:
- eigen_diag: float32 [29568, 8192], P('col', 'row')
The draws below stay inside these ranges and needn't reach their ends.
Inputs may be any that keep to these rules, and one draw needn't show every extreme that they name: `seq_lengths`: the 8 lengths sum to 512 and the longest is exactly 256.
All inputs are finite; a program needn't handle non-finite values.
Results may differ from the reference program's by a relative error of at most 0.0037.
Values may be sent and summed in bfloat16 or wider, within the bound.
A program may use at most 64 MiB of HBM per device.

```python
import math
import jax
import jax.numpy as jnp
import numpy as np
from jax import lax

D = 8192
FF = 29568
TOKENS = 512
SEQS = 8
MAXLEN = 256


def level_of(own_key, extent, shards, least, top_value):
    loudness, own = 1.0, jax.random.fold_in(own_key, 6)
    for dim, blocks in shards:
        heights = jnp.exp(jax.random.uniform(jax.random.fold_in(own, dim), (blocks,), jnp.float32, least / len(shards), top_value / len(shards)))
        loudness = loudness * jnp.repeat(heights, extent[dim] // blocks).reshape([-1 if axis == dim else 1 for axis in range(len(extent))])
    return loudness


def split_up(number_of, total, most, lean):
    weights = [(1 << 20) // math.isqrt(grade ** lean) + 1 for grade in range(2, number_of + 1)]
    rest, holding = total - most - (number_of - 1), [1] * (number_of - 1)
    while rest > 0:
        candidates = [i for i in range(number_of - 1) if holding[i] < most]
        mass, left = sum([weights[i] for i in candidates]), rest
        for i in candidates:
            extra = min(most - holding[i], max(1, left * weights[i] // mass), rest)
            holding[i] = holding[i] + extra
            rest = rest - extra
    return np.array([most] + holding)


def ragged(key, number_of, total, most, slope):
    if number_of == 2:
        one = jax.random.randint(key, (), max(1, total - most), min(most, total - 1) + 1)
        return jnp.stack([one, total - one])
    sizes = jnp.asarray(split_up(number_of, total, most, slope), jnp.int32)
    couples = (number_of - 1) // 2
    source_of, sink = sizes[1:1 + 2 * couples:2], sizes[2:2 + 2 * couples:2]
    slack = jnp.minimum(source_of - 1, most - sink)
    moved = jax.random.randint(jax.random.fold_in(key, 1), (couples,), 0, 1 << 20) % (slack + 1)
    sizes = sizes.at[1:1 + 2 * couples:2].set(source_of - moved).at[2:2 + 2 * couples:2].set(sink + moved)
    return sizes[jax.random.permutation(jax.random.fold_in(key, 2), number_of)]


def normal_values(key, dims, scale, most, pieces=(), held_as=jnp.bfloat16):
    factor_of = level_of(key, dims, pieces, -0.22, 0.18) if pieces else 1.0
    drawn = jax.random.normal(key, dims, jnp.float32) * scale * factor_of
    return jnp.minimum(jnp.maximum(drawn, -most), most).astype(held_as)


def setup_inputs(seed: int = 0) -> dict:
    arg_keys = jax.random.split(jax.random.key(seed), 6)
    return {
        "activations": normal_values(arg_keys[0], (TOKENS, D), 1.0, 6.0, ((0, 16), (1, 16))),
        "out_grads": normal_values(arg_keys[1], (TOKENS, FF), 1.0, 6.0, ((0, 16), (1, 16))),
        "basis_in": normal_values(arg_keys[2], (D, D), D ** -0.5, 0.0625, ((0, 16), (1, 16))),
        "basis_out": normal_values(arg_keys[3], (FF, FF), FF ** -0.5, 0.03125, ((0, 16), (1, 16))),
        "seq_lengths": ragged(arg_keys[4], SEQS, TOKENS, MAXLEN, 2).astype(jnp.int32),
    }


def reference(activations, out_grads, basis_in, basis_out, seq_lengths):
    rotated_acts = jnp.dot(activations, basis_in, preferred_element_type=jnp.float32).astype(jnp.bfloat16)
    rotated_grads = jnp.dot(out_grads, basis_out, preferred_element_type=jnp.float32).astype(jnp.bfloat16)
    offsets = (jnp.cumsum(seq_lengths) - seq_lengths).astype(jnp.int32)
    maxlen = TOKENS // 2
    acts_pad = jnp.concatenate([rotated_acts, jnp.zeros((maxlen, D), jnp.bfloat16)], axis=0)
    grads_pad = jnp.concatenate([rotated_grads, jnp.zeros((maxlen, FF), jnp.bfloat16)], axis=0)
    total = jnp.zeros((FF, D), jnp.float32)
    for index in range(SEQS):
        start = offsets[index].astype(jnp.int32)
        keep = (jnp.arange(maxlen) < seq_lengths[index]).astype(jnp.bfloat16)[:, None]
        act_block = lax.dynamic_slice_in_dim(acts_pad, start, maxlen, 0) * keep
        grad_block = lax.dynamic_slice_in_dim(grads_pad, start, maxlen, 0)
        product = lax.dot_general(grad_block, act_block, (((0,), (0,)), ((), ())), preferred_element_type=jnp.float32)
        total = total + product * product
    return total / TOKENS
```

```python
import functools

import jax
import jax.numpy as jnp
from jax import lax
from jax.experimental import pallas as pl
from jax.experimental.pallas import tpu as pltpu
from jax.sharding import PartitionSpec as P

MESH = pl.DeviceIdType.MESH
F32, BF16 = jnp.float32, jnp.bfloat16
NZ, NY, NX = 8, 4, 4
PLUS, MINUS = 0, 1


def comm_kernel(act, grad, basis_in, basis_out, rg_out, ra_out,
                gbuf, bo, part, psend, sib, rsend, rrecv, rg,
                abuf, bi, apart, arecv, ra,
                lsem, g_send, g_recv, sib_send, sib_recv, rs_send, rs_recv,
                ag_send, ag_recv, agx_send, agx_recv,
                az_send, az_recv, ax_send, ax_recv, ar_send, ar_recv, aa_send, aa_recv):
    row, col = lax.axis_index("row"), lax.axis_index("col")
    z, k = row // 2, row % 2
    y, x = col // 4, col % 4

    def dev(z=z, k=k, y=y, x=x):
        return {"row": z * 2 + k, "col": y * 4 + x}

    def zrel(d):
        return (z + (d + NZ)) % NZ

    def xyrel(dy, dx):
        return (y + dy + NY) % NY, (x + dx + NX) % NX

    pending = []

    def remote(src, dst, ssem, rsem, to):
        copy = pltpu.make_async_remote_copy(
            src_ref=src, dst_ref=dst, send_sem=ssem, recv_sem=rsem,
            device_id=to, device_id_type=MESH)
        copy.start()
        pending.append(copy)

    def arrived(dst, ssem, rsem):
        pltpu.make_async_remote_copy(
            src_ref=dst, dst_ref=dst, send_sem=ssem, recv_sem=rsem,
            device_id=dev(), device_id_type=MESH).wait_recv()

    loads = {}
    for index, (name, src, dst) in enumerate((
            ("ga", grad.at[pl.ds(0, 16)], gbuf.at[0, pl.ds(0, 16)]),
            ("gb", grad.at[pl.ds(16, 16)], gbuf.at[0, pl.ds(64, 16)]),
            ("act", act, abuf.at[row]),
            ("bi", basis_in, bi),
            ("bo", basis_out, bo))):
        loads[name] = pltpu.make_async_copy(src, dst, lsem.at[index])
        loads[name].start()

    peers = [dev(z=zrel(d)) for d in range(1, NZ)]
    peers += [dev(k=1 - k)]
    for i in range(1, 16):
        py, px = xyrel(i // 4, i % 4)
        peers.append(dev(y=py, x=px))
    barrier = pltpu.get_barrier_semaphore()
    for peer in peers:
        pl.semaphore_signal(barrier, inc=1, device_id=peer, device_id_type=MESH)
    pl.semaphore_wait(barrier, len(peers))

    def gslot(e, j):
        return gbuf.at[e, pl.ds(16 * j, 16)]

    counter = [0]

    def gsend(src, e, j, to):
        remote(src, gslot(e, j), g_send.at[counter[0]], g_recv.at[e, j], to)
        counter[0] += 1

    def garrived(e, j):
        arrived(gslot(e, j), g_send.at[0], g_recv.at[e, j])

    def xy(dy, dx):
        py, px = xyrel(dy, dx)
        return dev(y=py, x=px)

    loads["ga"].wait()
    loads["gb"].wait()
    for d in (1, 3, 2):
        gsend(gslot(0, 0), 0, d, xy(0, -d))
        gsend(gslot(0, 4), 0, 4 + d, xy(-d, 0))
    gsend(gslot(0, 0), 1, 0, xy(-1, 0))
    gsend(gslot(0, 0), 3, 0, xy(1, 0))
    gsend(gslot(0, 4), 1, 4, xy(0, -1))
    gsend(gslot(0, 4), 3, 4, xy(0, 1))

    loads["act"].wait()
    for i, d in enumerate((1, 7, 2, 6, 3, 5, 4)):
        remote(abuf.at[row], abuf.at[row], az_send.at[d], az_recv.at[d], dev(z=zrel(-d)))
    remote(abuf.at[row], abuf.at[row], ax_send.at[0], ax_recv.at[0], dev(k=1 - k))

    for d in (1, 3, 2):
        garrived(0, d)
        gsend(gslot(0, d), 1, d, xy(-1, 0))
        gsend(gslot(0, d), 3, d, xy(1, 0))
        garrived(0, 4 + d)
        gsend(gslot(0, 4 + d), 1, 4 + d, xy(0, -1))
        gsend(gslot(0, 4 + d), 3, 4 + d, xy(0, 1))

    def far(e, j):
        garrived(e, j)
        step = -1 if e == 1 else 1
        gsend(gslot(e, j), 2, j, xy(step, 0) if j < 4 else xy(0, step))

    far(1, 0)
    far(1, 4)

    def product(e, m):
        for lo, hi in ((0, 512), (512, 1024), (1024, 1536), (1536, 1848)):
            value = jnp.dot(gbuf[e], bo[:, lo:hi], preferred_element_type=F32)
            if m != 1:
                part[m, :, lo:hi] = value
            if m != 2:
                psend[m, :, lo:hi] = value.astype(BF16)

    loads["bo"].wait()
    product(0, 0)

    sibling = dev(k=1 - k)

    def give(m, slot):
        remote(psend.at[m], sib.at[slot], sib_send.at[slot], sib_recv.at[slot], sibling)

    def give_when(which, m, slot):
        @pl.when(k == which)
        def _():
            pltpu.make_async_remote_copy(
                src_ref=psend.at[m], dst_ref=sib.at[slot], send_sem=sib_send.at[slot],
                recv_sem=sib_recv.at[slot], device_id=sibling, device_id_type=MESH).start()

    give_when(1, 0, 0)

    def chunk_of(slot):
        return jnp.where(k == 0, 0, 2) if slot == 0 else jnp.where(k == 0, 1, 3)

    def part_of(slot):
        return jnp.where(k == 0, 0, 3) if slot == 0 else 2

    def own(slot, j):
        at = pl.ds(pl.multiple_of(16 * j, 16), 16)
        return part[part_of(slot), at, :] + sib[slot, at, :].astype(F32)

    def long_way(slot):
        return PLUS if slot == 0 else MINUS

    def rs_hop(slot, way, hop):
        sign = 1 if way == PLUS else -1
        first = 0 if way == long_way(slot) else 1
        if hop < first:
            return
        value = own(slot, zrel(sign * (4 - hop)))
        if hop > first:
            arrived(rrecv.at[slot, way, hop - 1], rs_send.at[slot, way, hop - 1], rs_recv.at[slot, way, hop - 1])
            value = value + rrecv[slot, way, hop - 1].astype(F32)
        rsend[slot, way, hop] = value.astype(BF16)
        remote(rsend.at[slot, way, hop], rrecv.at[slot, way, hop],
               rs_send.at[slot, way, hop], rs_recv.at[slot, way, hop], dev(z=zrel(sign)))

    def block_of(slot, j):
        e = chunk_of(slot)
        first = 2 * (((y + e) % 4) * 4 + (x + j) % 4)
        second = 2 * (((y + j) % 4) * 4 + (x + e) % 4) + 1
        return jnp.where(j < 4, first, second)

    def rs_end(slot):
        value = own(slot, z)
        for way in (PLUS, MINUS):
            arrived(rrecv.at[slot, way, 3], rs_send.at[slot, way, 3], rs_recv.at[slot, way, 3])
            value = value + rrecv[slot, way, 3].astype(F32)
        rg[block_of(slot, z)] = value.astype(BF16)

    def to_sibling(slot, d):
        at = rg.at[block_of(slot, zrel(d))]
        remote(at, at, agx_send.at[slot, d % NZ], agx_recv.at[slot, d % NZ], sibling)

    def from_sibling(slot, d):
        e = jnp.where(k == 0, 2, 0) if slot == 0 else jnp.where(k == 0, 3, 1)
        j = zrel(d)
        first = 2 * (((y + e) % 4) * 4 + (x + j) % 4)
        second = 2 * (((y + j) % 4) * 4 + (x + e) % 4) + 1
        at = rg.at[jnp.where(j < 4, first, second)]
        arrived(at, agx_send.at[slot, d % NZ], agx_recv.at[slot, d % NZ])

    def ag_hop(slot, way, hop):
        sign = 1 if way == PLUS else -1
        last = 4 if way == long_way(slot) else 3
        if hop > last:
            return
        at = rg.at[block_of(slot, zrel(-sign * hop))]
        if hop > 0:
            arrived(at, ag_send.at[slot, way, hop - 1], ag_recv.at[slot, way, hop - 1])
        if hop < last:
            remote(at, at, ag_send.at[slot, way, hop], ag_recv.at[slot, way, hop], dev(z=zrel(sign)))
        if hop > 0:
            to_sibling(slot, -sign * hop)

    def ag_both(slot, hop):
        ag_hop(slot, PLUS, hop)
        ag_hop(slot, MINUS, hop)
        if hop == 0:
            to_sibling(slot, 0)

    def rs_both(slot, hop):
        rs_hop(slot, PLUS, hop)
        rs_hop(slot, MINUS, hop)

    for j in (1, 5):
        far(1, j)
    for j in (2, 3, 6, 7):
        far(3, j)
    for j in (2, 3, 6, 7):
        garrived(1, j)
    for j in (0, 1, 4, 5):
        garrived(3, j)

    for d in range(1, NZ):
        r = zrel(d) * 2 + k
        arrived(abuf.at[r], az_send.at[d], az_recv.at[d])
        remote(abuf.at[r], abuf.at[r], ax_send.at[d], ax_recv.at[d], sibling)

    product(jnp.where(k == 0, 3, 1), 1)
    give(1, 1)
    product(jnp.where(k == 0, 1, 3), 2)
    arrived(sib.at[1], sib_send.at[1], sib_recv.at[1])
    rs_both(1, 0)
    for j in range(8):
        garrived(2, j)
    product(2, 3)
    give_when(0, 3, 0)
    rs_both(1, 1)
    arrived(sib.at[0], sib_send.at[0], sib_recv.at[0])
    rs_both(0, 0)

    loads["bi"].wait()
    for d in range(NZ):
        arrived(abuf.at[zrel(d) * 2 + 1 - k], ax_send.at[d], ax_recv.at[d])
    for lo in range(0, 16, 4):
        value = jnp.dot(abuf[lo:lo + 4].reshape(128, 512), bi[...], preferred_element_type=F32)
        apart[lo:lo + 4] = value.reshape(4, 32, 512)
    for i in range(1, 16):
        py, px = xyrel(-(i // 4), -(i % 4))
        remote(apart.at[py * 4 + px], arecv.at[i], ar_send.at[i], ar_recv.at[i], dev(y=py, x=px))

    rs_both(1, 2)
    rs_both(0, 1)
    rs_both(1, 3)
    rs_both(0, 2)
    rs_end(1)
    ag_both(1, 0)
    rs_both(0, 3)
    ag_both(1, 1)
    rs_end(0)
    ag_both(0, 0)
    ag_both(1, 2)

    value = apart[col]
    for i in range(1, 16):
        arrived(arecv.at[i], ar_send.at[i], ar_recv.at[i])
        value = value + arecv[i]
    ra[col] = value.astype(BF16)
    for i in range(1, 16):
        py, px = xyrel(-(i // 4), -(i % 4))
        remote(ra.at[col], ra.at[col], aa_send.at[i], aa_recv.at[i], dev(y=py, x=px))

    ag_both(0, 1)
    ag_both(1, 3)
    ag_both(0, 2)
    ag_both(1, 4)
    ag_both(0, 3)
    ag_both(0, 4)

    for i in range(1, 16):
        py, px = xyrel(i // 4, i % 4)
        arrived(ra.at[py * 4 + px], aa_send.at[i], aa_recv.at[i])
    ra_copy = pltpu.make_async_copy(ra, ra_out, lsem.at[0])
    ra_copy.start()
    for slot in (1, 0):
        for d in (0, 1, 7, 2, 6, 3, 5, 4):
            from_sibling(slot, d)
    rg_copy = pltpu.make_async_copy(rg, rg_out, lsem.at[1])
    rg_copy.start()
    for copy in pending:
        copy.wait_send()
    pltpu.make_async_remote_copy(
        src_ref=psend.at[0], dst_ref=sib.at[0], send_sem=sib_send.at[0],
        recv_sem=sib_recv.at[0], device_id=sibling, device_id_type=MESH).wait_send()
    ra_copy.wait()
    rg_copy.wait()


def gathered(activations, out_grads, basis_in, basis_out):
    ff, d = basis_out.shape[1], basis_in.shape[1]
    vmem, dma = pltpu.VMEM, pltpu.SemaphoreType.DMA
    any_ = pl.BlockSpec(memory_space=pl.ANY)
    return pl.pallas_call(
        comm_kernel,
        out_shape=(jax.ShapeDtypeStruct((32, 16, ff), BF16), jax.ShapeDtypeStruct((16, 32, d), BF16)),
        in_specs=[any_] * 4,
        out_specs=(any_, any_),
        scratch_shapes=[
            vmem((4, 128, ff), BF16), vmem((ff, ff), BF16), vmem((4, 128, ff), F32),
            vmem((4, 128, ff), BF16), vmem((2, 128, ff), BF16),
            vmem((2, 2, 4, 16, ff), BF16), vmem((2, 2, 4, 16, ff), BF16), vmem((32, 16, ff), BF16),
            vmem((16, 32, d), BF16), vmem((d, d), BF16), vmem((16, 32, d), F32), vmem((16, 32, d), F32),
            vmem((16, 32, d), BF16),
            dma((5,)), dma((30,)), dma((4, 8)), dma((2,)), dma((2,)), dma((2, 2, 4)), dma((2, 2, 4)),
            dma((2, 2, 4)), dma((2, 2, 4)), dma((2, 8)), dma((2, 8)),
            dma((8,)), dma((8,)), dma((8,)), dma((8,)), dma((16,)), dma((16,)), dma((16,)), dma((16,)),
        ],
        compiler_params=pltpu.CompilerParams(
            collective_id=0, has_side_effects=True, vmem_limit_bytes=56 << 20),
        name="gather_rotate",
    )(activations, out_grads, basis_in, basis_out)


TILE = 384


def diag_kernel(bounds, rg, ra, out, gt):
    gt[...] = rg[...].T
    out[...] = jnp.zeros_like(out)

    def one(s, carry):
        start, end = bounds[s], bounds[s + 1]

        def window(w):
            base = pl.multiple_of(w * 256, 256)
            token = base + lax.broadcasted_iota(jnp.int32, (256, 1), 0)
            keep = (token >= start) & (token < end)
            block = ra[pl.ds(base, 256), :]
            block = jnp.where(keep, block, jnp.zeros_like(block))
            return jnp.dot(gt[:, pl.ds(base, 256)], block, preferred_element_type=F32)

        both = (start < 256) & (end > 256)

        @pl.when(jnp.logical_not(both))
        def _():
            p = window(jnp.where(start < 256, 0, 1))
            out[...] += p * p

        @pl.when(both)
        def _():
            p = window(0) + window(1)
            out[...] += p * p

        return carry

    lax.fori_loop(0, 8, one, 0)
    out[...] = out[...] * (1.0 / 512.0)


def diagonal(bounds, rg, ra):
    tokens, ff = rg.shape
    d = ra.shape[1]
    return pl.pallas_call(
        diag_kernel,
        out_shape=jax.ShapeDtypeStruct((ff, d), F32),
        grid_spec=pltpu.PrefetchScalarGridSpec(
            num_scalar_prefetch=1,
            grid=(pl.cdiv(ff, TILE),),
            in_specs=[
                pl.BlockSpec((tokens, TILE), lambda i, b: (0, i)),
                pl.BlockSpec((tokens, d), lambda i, b: (0, 0)),
            ],
            out_specs=pl.BlockSpec((TILE, d), lambda i, b: (i, 0)),
            scratch_shapes=[pltpu.VMEM((TILE, tokens), BF16)],
        ),
        compiler_params=pltpu.CompilerParams(vmem_limit_bytes=40 << 20),
        name="eigen_diagonal",
    )(bounds, rg, ra)


def local(activations, out_grads, basis_in, basis_out, seq_lengths):
    rg, ra = gathered(activations, out_grads, basis_in, basis_out)
    bounds = jnp.concatenate([jnp.zeros((1,), jnp.int32), jnp.cumsum(seq_lengths)]).astype(jnp.int32)
    rg = rg.reshape(512, rg.shape[-1])
    ra = ra.reshape(512, ra.shape[-1])
    return diagonal(bounds, rg, ra)


def solution(mesh):
    in_specs = (P("row", "col"), P("col", "row"), P("col", "row"), P("row", "col"), P())
    out_specs = P("col", "row")
    return jax.shard_map(local, mesh=mesh, in_specs=in_specs, out_specs=out_specs, check_vma=False)
```

```python
import jax
import jax.numpy as jnp
from jax import lax
from jax.experimental import pallas as pl
from jax.experimental.pallas import tpu as pltpu
from jax.sharding import PartitionSpec as P

MESH = pl.DeviceIdType.MESH
F32, BF16 = jnp.float32, jnp.bfloat16
NZ, NY, NX = 8, 4, 4
PLUS, MINUS = 0, 1


def comm_kernel(act, grad, basis_in, basis_out, rg, ra,
                gbuf, bo, part, psend, sib, rsend, rrecv,
                abuf, bi, apart, arecv,
                lsem, g_send, g_recv, sib_send, sib_recv, rs_send, rs_recv,
                ag_send, ag_recv, agx_send, agx_recv,
                az_send, az_recv, ax_send, ax_recv, ar_send, ar_recv, aa_send, aa_recv):
    row, col = lax.axis_index("row"), lax.axis_index("col")
    z, k = row // 2, row % 2
    y, x = col // 4, col % 4

    def dev(z=z, k=k, y=y, x=x):
        return {"row": z * 2 + k, "col": y * 4 + x}

    def zrel(d):
        return (z + (d + NZ)) % NZ

    def xyrel(dy, dx):
        return (y + dy + NY) % NY, (x + dx + NX) % NX

    def remote(src, dst, ssem, rsem, to):
        pltpu.make_async_remote_copy(
            src_ref=src, dst_ref=dst, send_sem=ssem, recv_sem=rsem,
            device_id=to, device_id_type=MESH).start()

    def arrived(dst, ssem, rsem):
        pltpu.make_async_remote_copy(
            src_ref=dst, dst_ref=dst, send_sem=ssem, recv_sem=rsem,
            device_id=dev(), device_id_type=MESH).wait_recv()

    def sent(src, ssem, rsem):
        pltpu.make_async_remote_copy(
            src_ref=src, dst_ref=src, send_sem=ssem, recv_sem=rsem,
            device_id=dev(), device_id_type=MESH).wait_send()

    inner, outer = k == 0, k == 1

    peers = [dev(z=zrel(d)) for d in range(1, NZ)]
    peers += [dev(k=1 - k)]
    for i in range(1, 16):
        py, px = xyrel(i // 4, i % 4)
        peers.append(dev(y=py, x=px))
    barrier = pltpu.get_barrier_semaphore()
    for peer in peers:
        pl.semaphore_signal(barrier, inc=1, device_id=peer, device_id_type=MESH)
    loads = {}
    for index, (name, src, dst) in enumerate((
            ("ga", grad.at[pl.ds(0, 16)], gbuf.at[0, pl.ds(0, 16)]),
            ("gb", grad.at[pl.ds(16, 16)], gbuf.at[0, pl.ds(64, 16)]),
            ("act", act, abuf.at[row]),
            ("bi", basis_in, bi),
            ("bo", basis_out, bo))):
        loads[name] = pltpu.make_async_copy(src, dst, lsem.at[index])
        loads[name].start()

    pl.semaphore_wait(barrier, len(peers))

    def gslot(e, j):
        return gbuf.at[e, pl.ds(16 * j, 16)]

    counter = [0]

    def gsend(src, e, j, to):
        remote(src, gslot(e, j), g_send.at[counter[0]], g_recv.at[e, j], to)
        counter[0] += 1

    def gsent():
        for i in range(30):
            sent(gslot(0, 0), g_send.at[i], g_recv.at[0, 0])

    def garrived(e, j):
        arrived(gslot(e, j), g_send.at[0], g_recv.at[e, j])

    def xy(dy, dx):
        py, px = xyrel(dy, dx)
        return dev(y=py, x=px)

    loads["ga"].wait()
    loads["gb"].wait()
    for d in (1, 3, 2):
        gsend(gslot(0, 0), 0, d, xy(0, -d))
        gsend(gslot(0, 4), 0, 4 + d, xy(-d, 0))
    gsend(gslot(0, 0), 1, 0, xy(-1, 0))
    gsend(gslot(0, 0), 3, 0, xy(1, 0))
    gsend(gslot(0, 4), 1, 4, xy(0, -1))
    gsend(gslot(0, 4), 3, 4, xy(0, 1))

    loads["act"].wait()
    for i, d in enumerate((1, 7, 2, 6, 3, 5, 4)):
        remote(abuf.at[row], abuf.at[row], az_send.at[d], az_recv.at[d], dev(z=zrel(-d)))
    remote(abuf.at[row], abuf.at[row], ax_send.at[0], ax_recv.at[0], dev(k=1 - k))

    for d in (1, 3, 2):
        garrived(0, d)
        gsend(gslot(0, d), 1, d, xy(-1, 0))
        gsend(gslot(0, d), 3, d, xy(1, 0))
        garrived(0, 4 + d)
        gsend(gslot(0, 4 + d), 1, 4 + d, xy(0, -1))
        gsend(gslot(0, 4 + d), 3, 4 + d, xy(0, 1))

    def far(e, j):
        garrived(e, j)
        step = -1 if e == 1 else 1
        gsend(gslot(e, j), 2, j, xy(step, 0) if j < 4 else xy(0, step))

    far(1, 0)
    far(1, 4)

    sibling = dev(k=1 - k)

    def product(e):
        for lo, hi in ((0, 512), (512, 1024), (1024, 1536), (1536, 1848)):
            value = jnp.dot(gbuf[e], bo[:, lo:hi], preferred_element_type=F32)

            @pl.when(inner)
            def _():
                psend[e, :, lo:hi] = value.astype(BF16)

            @pl.when(outer)
            def _():
                part[e, :, lo:hi] = value

        @pl.when(inner)
        def _():
            remote(psend.at[e], sib.at[e], sib_send.at[e], sib_recv.at[e], sibling)

    def own(e, j):
        at = pl.ds(pl.multiple_of(16 * j, 16), 16)
        return part[e, at, :] + sib[e, at, :].astype(F32)

    def long_way(e):
        return PLUS if e < 2 else MINUS

    def rs_send_own(e, way, index, to_owner, to):
        sign = 1 if way == PLUS else -1
        rsend[e, way, index] = own(e, zrel(sign * to_owner)).astype(BF16)
        remote(rsend.at[e, way, index], rrecv.at[e, way, index],
               rs_send.at[e, way, index], rs_recv.at[e, way, index], dev(z=zrel(sign * to)))

    def rs_take(e, way, index):
        arrived(rrecv.at[e, way, index], rs_send.at[e, way, index], rs_recv.at[e, way, index])
        return rrecv[e, way, index].astype(F32)

    def rs_start(e):
        rs_send_own(e, long_way(e), 1, 4, 2)
        for way in (long_way(e), 1 - long_way(e)):
            rs_send_own(e, way, 0, 3, 1)
        for way in (long_way(e), 1 - long_way(e)):
            rs_send_own(e, way, 2, 1, 1)

    def rs_relay(e):
        for way in (long_way(e), 1 - long_way(e)):
            sign = 1 if way == PLUS else -1
            value = own(e, zrel(sign * 2)) + rs_take(e, way, 0)
            if way == long_way(e):
                value = value + rs_take(e, way, 1)
            rsend[e, way, 3] = value.astype(BF16)
            remote(rsend.at[e, way, 3], rrecv.at[e, way, 3],
                   rs_send.at[e, way, 3], rs_recv.at[e, way, 3], dev(z=zrel(sign * 2)))

    def block_of(e, j):
        first = 2 * (((y + e) % 4) * 4 + (x + j) % 4)
        second = 2 * (((y + j) % 4) * 4 + (x + e) % 4) + 1
        return jnp.where(j < 4, first, second)

    def rs_end(e):
        value = own(e, z)
        for index in (2, 3):
            for way in (PLUS, MINUS):
                value = value + rs_take(e, way, index)
        rg[block_of(e, z)] = value.astype(BF16)

    def over(e, d):
        at = rg.at[block_of(e, zrel(d))]
        remote(at, at, agx_send.at[e, d % NZ], agx_recv.at[e, d % NZ], sibling)

    def ag_hop(e, way, hop):
        sign = 1 if way == PLUS else -1
        last = 4 if way == long_way(e) else 3
        if hop > last:
            return
        at = rg.at[block_of(e, zrel(-sign * hop))]
        if hop > 0:
            arrived(at, ag_send.at[e, way, hop - 1], ag_recv.at[e, way, hop - 1])
        if hop < last:
            remote(at, at, ag_send.at[e, way, hop], ag_recv.at[e, way, hop], dev(z=zrel(sign)))

    def ag_over(e, way, hop):
        if hop <= (4 if way == long_way(e) else 3) and (hop > 0 or way == PLUS):
            over(e, (-1 if way == PLUS else 1) * hop)

    def stage(e, n):
        if n == 0:
            arrived(sib.at[e], sib_send.at[e], sib_recv.at[e])
            rs_start(e)
            return
        if n == 1:
            rs_relay(e)
            return
        if n == 2:
            rs_end(e)
        for act in (ag_hop, ag_over):
            for way in (long_way(e), 1 - long_way(e)):
                act(e, way, n - 2)

    def stages(*todo):
        @pl.when(outer)
        def _():
            for e, n in todo:
                stage(e, n)

    def acts_over():
        for d in range(1, NZ):
            r = zrel(d) * 2 + k
            arrived(abuf.at[r], az_send.at[d], az_recv.at[d])
            remote(abuf.at[r], abuf.at[r], ax_send.at[d], ax_recv.at[d], sibling)

    def acts_product():
        loads["bi"].wait()
        for d in range(NZ):
            arrived(abuf.at[zrel(d) * 2 + 1 - k], ax_send.at[d], ax_recv.at[d])
        for lo in range(0, 16, 4):
            value = jnp.dot(abuf[lo:lo + 4].reshape(128, 512), bi[...], preferred_element_type=F32)
            apart[lo:lo + 4] = value.reshape(4, 32, 512)
        for i in range(1, 16):
            py, px = xyrel(-(i // 4), -(i % 4))
            remote(apart.at[py * 4 + px], arecv.at[i], ar_send.at[i], ar_recv.at[i], dev(y=py, x=px))

    def acts_sum():
        value = apart[col]
        for i in range(1, 16):
            arrived(arecv.at[i], ar_send.at[i], ar_recv.at[i])
            value = value + arecv[i]
        ra[col] = value.astype(BF16)
        for i in range(1, 16):
            py, px = xyrel(-(i // 4), -(i % 4))
            remote(ra.at[col], ra.at[col], aa_send.at[i], aa_recv.at[i], dev(y=py, x=px))

    def acts_end():
        for i in range(1, 16):
            py, px = xyrel(i // 4, i % 4)
            arrived(ra.at[py * 4 + px], aa_send.at[i], aa_recv.at[i])

    loads["bo"].wait()
    product(0)
    for j in (1, 5):
        far(1, j)
    for j in (2, 3, 6, 7):
        far(3, j)
    stages((0, 0))
    for j in (2, 3, 6, 7):
        garrived(1, j)
    product(1)
    for j in (0, 1, 4, 5):
        garrived(3, j)
    product(3)
    stages((0, 1), (1, 0), (3, 0))
    acts_over()
    stages((0, 2))
    for j in range(8):
        garrived(2, j)
    product(2)
    stages((1, 1), (3, 1), (0, 3), (2, 0))
    acts_product()
    stages((1, 2), (3, 2), (0, 4), (2, 1))
    stages((1, 3), (3, 3), (0, 5), (2, 2))
    stages((1, 4), (3, 4), (0, 6), (2, 3))
    acts_sum()
    stages((1, 5), (3, 5), (2, 4))
    stages((1, 6), (3, 6), (2, 5))
    stages((2, 6))
    acts_end()

    @pl.when(inner)
    def _():
        for e in (0, 1, 3, 2):
            for d in (0, 1, 7, 2, 6, 3, 5, 4):
                arrived(rg.at[block_of(e, zrel(d))], agx_send.at[e, d], agx_recv.at[e, d])
            sent(psend.at[e], sib_send.at[e], sib_recv.at[e])

    @pl.when(outer)
    def _():
        for e in range(4):
            for way in (PLUS, MINUS):
                for hop in ((0, 1, 2, 3) if way == long_way(e) else (0, 2, 3)):
                    sent(rsend.at[e, way, hop], rs_send.at[e, way, hop], rs_recv.at[e, way, hop])
                for hop in range(4 if way == long_way(e) else 3):
                    sent(rg.at[0], ag_send.at[e, way, hop], ag_recv.at[e, way, hop])
            for d in range(NZ):
                sent(rg.at[0], agx_send.at[e, d], agx_recv.at[e, d])

    gsent()
    for d in range(NZ):
        if d:
            sent(abuf.at[0], az_send.at[d], az_recv.at[d])
        sent(abuf.at[0], ax_send.at[d], ax_recv.at[d])
    for i in range(1, 16):
        sent(apart.at[0], ar_send.at[i], ar_recv.at[i])
        sent(ra.at[0], aa_send.at[i], aa_recv.at[i])


def gathered(activations, out_grads, basis_in, basis_out):
    ff, d = basis_out.shape[1], basis_in.shape[1]
    vmem, dma = pltpu.VMEM, pltpu.SemaphoreType.DMA
    any_ = pl.BlockSpec(memory_space=pltpu.HBM)
    inside = pl.BlockSpec(memory_space=pltpu.VMEM)
    return pl.pallas_call(
        comm_kernel,
        out_shape=(vmem((32, 16, ff), BF16), vmem((16, 32, d), BF16)),
        in_specs=[any_] * 4,
        out_specs=(inside, inside),
        scratch_shapes=[
            vmem((4, 128, ff), BF16), vmem((ff, ff), BF16), vmem((4, 128, ff), F32),
            vmem((4, 128, ff), BF16), vmem((4, 128, ff), BF16),
            vmem((4, 2, 4, 16, ff), BF16), vmem((4, 2, 4, 16, ff), BF16),
            vmem((16, 32, d), BF16), vmem((d, d), BF16), vmem((16, 32, d), F32), vmem((16, 32, d), F32),
            dma((5,)), dma((30,)), dma((4, 8)), dma((4,)), dma((4,)), dma((4, 2, 4)), dma((4, 2, 4)),
            dma((4, 2, 4)), dma((4, 2, 4)), dma((4, 8)), dma((4, 8)),
            dma((8,)), dma((8,)), dma((8,)), dma((8,)), dma((16,)), dma((16,)), dma((16,)), dma((16,)),
        ],
        compiler_params=pltpu.CompilerParams(
            collective_id=0, has_side_effects=True, vmem_limit_bytes=60 << 20),
        name="gather_rotate",
    )(activations, out_grads, basis_in, basis_out)


TILES = ((0, 512), (512, 1024), (1024, 1536), (1536, 1848))


def diag_kernel(lens, rg, ra, out_hbm, out, masked, sem):
    starts, total = [], 0
    for s in range(8):
        starts.append(total)
        total = total + lens[s]
    longest, begin, most = 0, 0, lens[0]
    for s in range(1, 8):
        more = lens[s] > most
        longest = jnp.where(more, s, longest)
        begin = jnp.where(more, starts[s], begin)
        most = jnp.where(more, lens[s], most)
    token = lax.broadcasted_iota(jnp.int32, (256, 1), 0)
    wraps = token < begin
    low, high = ra[0:256, :], ra[256:512, :]
    masked[0] = jnp.where(wraps, high, low)
    others = jnp.where(wraps, low, high)
    for i in range(7):
        before = i < longest
        start = jnp.where(before, starts[i], starts[i + 1])
        length = jnp.where(before, lens[i], lens[i + 1])
        start = jnp.where(start >= 256, start - 256, start)
        keep = (token >= start) & (token < start + length)
        masked[i + 1] = jnp.where(keep, others, jnp.zeros_like(others))
    copies = []
    for index, (lo, hi) in enumerate(TILES):
        low, high = rg[0:256, lo:hi], rg[256:512, lo:hi]
        long_side = jnp.where(wraps, high, low).T
        other_side = jnp.where(wraps, low, high).T
        for i in range(8):
            p = jnp.dot(long_side if i == 0 else other_side, masked[i], preferred_element_type=F32)
            if i == 0:
                out[lo:hi, :] = p * p
            elif i < 7:
                out[lo:hi, :] += p * p
            else:
                out[lo:hi, :] = (out[lo:hi, :] + p * p) * (1.0 / 512.0)
        copies.append(pltpu.make_async_copy(
            out.at[pl.ds(lo, hi - lo)], out_hbm.at[pl.ds(lo, hi - lo)], sem.at[index]))
        copies[-1].start()
    for copy in copies:
        copy.wait()


def diagonal(lens, rg, ra):
    ff, d = rg.shape[1], ra.shape[1]
    inside = pl.BlockSpec(memory_space=pltpu.VMEM)
    return pl.pallas_call(
        diag_kernel,
        out_shape=jax.ShapeDtypeStruct((ff, d), F32),
        in_specs=[pl.BlockSpec(memory_space=pltpu.SMEM), inside, inside],
        out_specs=pl.BlockSpec(memory_space=pl.ANY),
        scratch_shapes=[
            pltpu.VMEM((ff, d), F32), pltpu.VMEM((8, 256, d), BF16), pltpu.SemaphoreType.DMA((4,))],
        compiler_params=pltpu.CompilerParams(vmem_limit_bytes=48 << 20),
        name="eigen_diagonal",
    )(lens, rg, ra)


def local(activations, out_grads, basis_in, basis_out, seq_lengths):
    rg, ra = gathered(activations, out_grads, basis_in, basis_out)
    rg = rg.reshape(512, rg.shape[-1])
    ra = ra.reshape(512, ra.shape[-1])
    return diagonal(seq_lengths, rg, ra)


def solution(mesh):
    in_specs = (P("row", "col"), P("col", "row"), P("col", "row"), P("row", "col"), P())
    out_specs = P("col", "row")
    return jax.shard_map(local, mesh=mesh, in_specs=in_specs, out_specs=out_specs, check_vma=False)
```

```python
import jax
import jax.numpy as jnp
from jax import lax
from jax.experimental import pallas as pl
from jax.experimental.pallas import tpu as pltpu
from jax.sharding import PartitionSpec as P

MESH = pl.DeviceIdType.MESH
F32, BF16 = jnp.float32, jnp.bfloat16
NZ, NY, NX = 8, 4, 4
PLUS, MINUS = 0, 1


def comm_kernel(act, grad, basis_in, basis_out, rg, ra,
                gbuf, bo, part, psend, sib, rsend, rrecv,
                abuf, bi, apart, arecv,
                lsem, g_send, g_recv, sib_send, sib_recv, rs_send, rs_recv,
                ag_send, ag_recv, agx_send, agx_recv,
                az_send, az_recv, ax_send, ax_recv, ar_send, ar_recv, aa_send, aa_recv):
    row, col = lax.axis_index("row"), lax.axis_index("col")
    z, k = row // 2, row % 2
    y, x = col // 4, col % 4

    def dev(z=z, k=k, y=y, x=x):
        return {"row": z * 2 + k, "col": y * 4 + x}

    def zrel(d):
        return (z + (d + NZ)) % NZ

    def xyrel(dy, dx):
        return (y + dy + NY) % NY, (x + dx + NX) % NX

    def remote(src, dst, ssem, rsem, to):
        pltpu.make_async_remote_copy(
            src_ref=src, dst_ref=dst, send_sem=ssem, recv_sem=rsem,
            device_id=to, device_id_type=MESH).start()

    def arrived(dst, ssem, rsem):
        pltpu.make_async_remote_copy(
            src_ref=dst, dst_ref=dst, send_sem=ssem, recv_sem=rsem,
            device_id=dev(), device_id_type=MESH).wait_recv()

    def sent(src, ssem, rsem):
        pltpu.make_async_remote_copy(
            src_ref=src, dst_ref=src, send_sem=ssem, recv_sem=rsem,
            device_id=dev(), device_id_type=MESH).wait_send()

    inner, outer = k == 0, k == 1

    peers = [dev(z=zrel(d)) for d in range(1, NZ)]
    peers += [dev(k=1 - k)]
    for i in range(1, 16):
        py, px = xyrel(i // 4, i % 4)
        peers.append(dev(y=py, x=px))
    barrier = pltpu.get_barrier_semaphore()
    for peer in peers:
        pl.semaphore_signal(barrier, inc=1, device_id=peer, device_id_type=MESH)
    loads = {}
    for index, (name, src, dst) in enumerate((
            ("ga", grad.at[pl.ds(0, 16)], gbuf.at[pl.ds(0, 16)]),
            ("gb", grad.at[pl.ds(16, 16)], gbuf.at[pl.ds(64, 16)]),
            ("act", act, abuf.at[row]),
            ("bi", basis_in, bi),
            ("bo", basis_out, bo))):
        loads[name] = pltpu.make_async_copy(src, dst, lsem.at[index])
        loads[name].start()

    pl.semaphore_wait(barrier, len(peers))

    def gslot(e, j):
        return gbuf.at[pl.ds(128 * e + 16 * j, 16)]

    def gsend(src, e, j, to):
        remote(src, gslot(e, j), g_send.at[0], g_recv.at[e, 0 if e == 2 else j], to)

    def gsent():
        sent(gbuf.at[pl.ds(0, 480)], g_send.at[0], g_recv.at[0, 0])

    def last_arrived():
        arrived(gbuf.at[pl.ds(256, 128)], g_send.at[0], g_recv.at[2, 0])

    def garrived(e, j):
        arrived(gslot(e, j), g_send.at[0], g_recv.at[e, j])

    def xy(dy, dx):
        py, px = xyrel(dy, dx)
        return dev(y=py, x=px)

    loads["ga"].wait()
    loads["gb"].wait()
    for d in (1, 3, 2):
        gsend(gslot(0, 0), 0, d, xy(0, -d))
        gsend(gslot(0, 4), 0, 4 + d, xy(-d, 0))
    gsend(gslot(0, 0), 1, 0, xy(-1, 0))
    gsend(gslot(0, 0), 3, 0, xy(1, 0))
    gsend(gslot(0, 4), 1, 4, xy(0, -1))
    gsend(gslot(0, 4), 3, 4, xy(0, 1))

    loads["act"].wait()
    for i, d in enumerate((1, 7, 2, 6, 3, 5, 4)):
        remote(abuf.at[row], abuf.at[row], az_send.at[0], az_recv.at[0], dev(z=zrel(-d)))
    remote(abuf.at[row], abuf.at[row], ax_send.at[0], ax_recv.at[0], dev(k=1 - k))

    for d in (1, 3, 2):
        garrived(0, d)
        gsend(gslot(0, d), 1, d, xy(-1, 0))
        gsend(gslot(0, d), 3, d, xy(1, 0))
        garrived(0, 4 + d)
        gsend(gslot(0, 4 + d), 1, 4 + d, xy(0, -1))
        gsend(gslot(0, 4 + d), 3, 4 + d, xy(0, 1))

    def far(e, j):
        garrived(e, j)
        step = -1 if e == 1 else 1
        gsend(gslot(e, j), 2, j, xy(step, 0) if j < 4 else xy(0, step))

    far(1, 0)
    far(1, 4)

    sibling = dev(k=1 - k)

    def product(e):
        for lo, hi in ((0, 512), (512, 1024), (1024, 1536), (1536, 1848)):
            value = jnp.dot(gbuf[128 * e:128 * e + 128], bo[:, lo:hi], preferred_element_type=F32)

            @pl.when(inner)
            def _():
                psend[e, :, lo:hi] = value.astype(BF16)

            @pl.when(outer)
            def _():
                part[e, :, lo:hi] = value

        @pl.when(inner)
        def _():
            remote(psend.at[e], sib.at[e], sib_send.at[0], sib_recv.at[e], sibling)

    def own(e, j):
        at = pl.ds(pl.multiple_of(16 * j, 16), 16)
        return part[e, at, :] + sib[e, at, :].astype(F32)

    def long_way(e):
        return PLUS if e < 2 else MINUS

    def rs_send_own(e, way, index, to_owner, to):
        sign = 1 if way == PLUS else -1
        rsend[8 * e + 4 * way + index] = own(e, zrel(sign * to_owner)).astype(BF16)
        remote(rsend.at[8 * e + 4 * way + index], rrecv.at[e, way, index],
               rs_send.at[0], rs_recv.at[e, way, index], dev(z=zrel(sign * to)))

    def rs_take(e, way, index):
        arrived(rrecv.at[e, way, index], rs_send.at[0], rs_recv.at[e, way, index])
        return rrecv[e, way, index].astype(F32)

    def rs_start(e):
        rs_send_own(e, long_way(e), 1, 4, 2)
        for way in (long_way(e), 1 - long_way(e)):
            rs_send_own(e, way, 0, 3, 1)
        for way in (long_way(e), 1 - long_way(e)):
            rs_send_own(e, way, 2, 1, 1)

    def rs_relay(e, way):
        sign = 1 if way == PLUS else -1
        value = own(e, zrel(sign * 2)) + rs_take(e, way, 0)
        if way == long_way(e):
            value = value + rs_take(e, way, 1)
        rsend[8 * e + 4 * way + 3] = value.astype(BF16)
        remote(rsend.at[8 * e + 4 * way + 3], rrecv.at[e, way, 3],
               rs_send.at[0], rs_recv.at[e, way, 3], dev(z=zrel(sign * 2)))

    def block_of(e, j):
        first = 2 * (((y + e) % 4) * 4 + (x + j) % 4)
        second = 2 * (((y + j) % 4) * 4 + (x + e) % 4) + 1
        return jnp.where(j < 4, first, second)

    def rs_end(e):
        value = own(e, z)
        for index in (2, 3):
            for way in (PLUS, MINUS):
                value = value + rs_take(e, way, index)
        rg[block_of(e, z)] = value.astype(BF16)

    def over(e, d):
        at = rg.at[block_of(e, zrel(d))]
        remote(at, at, agx_send.at[0], agx_recv.at[e], sibling)

    def ag_hop(e, way, hop):
        sign = 1 if way == PLUS else -1
        last = 4 if way == long_way(e) else 3
        if hop > last:
            return
        at = rg.at[block_of(e, zrel(-sign * hop))]
        if hop > 0:
            arrived(at, ag_send.at[0], ag_recv.at[e, way, hop - 1])
        if hop < last:
            remote(at, at, ag_send.at[0], ag_recv.at[e, way, hop], dev(z=zrel(sign)))

    def ag_send_block(e, way, index, d, to):
        sign = 1 if way == PLUS else -1
        at = rg.at[block_of(e, zrel(d))]
        remote(at, at, ag_send.at[0], ag_recv.at[e, way, index], dev(z=zrel(sign * to)))

    def ag_take(e, way, index, d):
        at = rg.at[block_of(e, zrel(d))]
        arrived(at, ag_send.at[0], ag_recv.at[e, way, index])

    def start(e):
        arrived(sib.at[e], sib_send.at[0], sib_recv.at[e])
        rs_start(e)

    def end(e):
        rs_end(e)
        ways = (long_way(e), 1 - long_way(e))
        if e == 0:
            for way in ways:
                ag_hop(e, way, 0)
        else:
            for index in (1, 0):
                for way in ways:
                    ag_send_block(e, way, index, 0, index + 1)
        over(e, 0)

    def hop(e, way, n):
        ag_hop(e, way, n)
        over(e, (-1 if way == PLUS else 1) * n)

    def forward(e, way):
        sign = 1 if way == PLUS else -1
        ag_take(e, way, 1, -2 * sign)
        if way == long_way(e):
            ag_send_block(e, way, 3, -2 * sign, 2)
        ag_send_block(e, way, 2, -2 * sign, 1)
        over(e, -2 * sign)

    def take(e, way, n):
        sign = 1 if way == PLUS else -1
        ag_take(e, way, {1: 0, 3: 2, 4: 3}[n], -n * sign)
        over(e, -n * sign)

    def steps(*todo):
        @pl.when(outer)
        def _():
            for act, *what in todo:
                act(*what)

    def acts_over():
        arrived(abuf.at[pl.ds(0, 7)], az_send.at[0], az_recv.at[0])
        for d in range(1, NZ):
            r = zrel(d) * 2 + k
            remote(abuf.at[r], abuf.at[r], ax_send.at[0], ax_recv.at[0], sibling)

    def acts_product():
        loads["bi"].wait()
        arrived(abuf.at[pl.ds(0, 8)], ax_send.at[0], ax_recv.at[0])
        for lo in range(0, 16, 4):
            value = jnp.dot(abuf[lo:lo + 4].reshape(128, 512), bi[...], preferred_element_type=F32)
            apart[lo:lo + 4] = value.reshape(4, 32, 512)
        for i in range(1, 16):
            py, px = xyrel(-(i // 4), -(i % 4))
            remote(apart.at[py * 4 + px], arecv.at[i], ar_send.at[0], ar_recv.at[0], dev(y=py, x=px))

    def acts_sum():
        value = apart[col]
        arrived(arecv.at[pl.ds(1, 15)], ar_send.at[0], ar_recv.at[0])
        for i in range(1, 16):
            value = value + arecv[i]
        ra[col] = value.astype(BF16)
        for i in range(1, 16):
            py, px = xyrel(-(i // 4), -(i % 4))
            remote(ra.at[col], ra.at[col], aa_send.at[0], aa_recv.at[0], dev(y=py, x=px))

    def acts_end():
        arrived(ra.at[pl.ds(0, 15)], aa_send.at[0], aa_recv.at[0])

    loads["bo"].wait()
    product(0)
    for j in (1, 5):
        far(1, j)
    for j in (2, 3, 6, 7):
        far(3, j)
    steps(
        (start, 0),
    )
    for j in (2, 3, 6, 7):
        garrived(1, j)
    product(1)
    for j in (0, 1, 4, 5):
        garrived(3, j)
    product(3)
    acts_over()
    steps(
        (rs_relay, 0, MINUS),
        (rs_relay, 0, PLUS),
        (start, 1),
    )
    last_arrived()
    product(2)
    steps(
        (start, 3),
        (end, 0),
        (rs_relay, 1, MINUS),
        (start, 2),
        (rs_relay, 1, PLUS),
        (rs_relay, 3, PLUS),
        (rs_relay, 3, MINUS),
        (hop, 0, PLUS, 1),
        (rs_relay, 2, PLUS),
    )
    acts_product()
    steps(
        (hop, 0, MINUS, 1),
        (end, 1),
        (rs_relay, 2, MINUS),
        (hop, 0, PLUS, 2),
        (end, 3),
        (hop, 0, MINUS, 2),
        (forward, 1, PLUS),
        (take, 1, PLUS, 1),
        (forward, 1, MINUS),
        (hop, 0, PLUS, 3),
        (take, 1, MINUS, 1),
        (end, 2),
        (forward, 3, PLUS),
        (take, 3, PLUS, 1),
        (forward, 3, MINUS),
    )
    acts_sum()
    steps(
        (take, 3, MINUS, 1),
        (hop, 0, MINUS, 3),
        (take, 1, PLUS, 4),
        (take, 1, PLUS, 3),
        (take, 1, MINUS, 3),
        (hop, 0, PLUS, 4),
        (forward, 2, MINUS),
        (take, 2, MINUS, 1),
        (forward, 2, PLUS),
        (take, 2, PLUS, 1),
        (take, 3, PLUS, 3),
        (take, 3, MINUS, 4),
        (take, 3, MINUS, 3),
        (take, 2, PLUS, 3),
        (take, 2, MINUS, 4),
        (take, 2, MINUS, 3),
    )
    acts_end()

    gsent()
    sent(abuf.at[pl.ds(0, 7)], az_send.at[0], az_recv.at[0])
    sent(abuf.at[pl.ds(0, 8)], ax_send.at[0], ax_recv.at[0])
    sent(apart.at[pl.ds(0, 15)], ar_send.at[0], ar_recv.at[0])
    sent(ra.at[pl.ds(0, 15)], aa_send.at[0], aa_recv.at[0])

    @pl.when(inner)
    def _():
        sent(psend, sib_send.at[0], sib_recv.at[0])
        for e in (0, 1, 3, 2):
            arrived(rg.at[pl.ds(8 * e, 8)], agx_send.at[0], agx_recv.at[e])

    @pl.when(outer)
    def _():
        sent(rsend.at[pl.ds(0, 28)], rs_send.at[0], rs_recv.at[0, 0, 0])
        sent(rg.at[pl.ds(0, 28)], ag_send.at[0], ag_recv.at[0, 0, 0])
        sent(rg, agx_send.at[0], agx_recv.at[0])


def gathered(activations, out_grads, basis_in, basis_out):
    ff, d = basis_out.shape[1], basis_in.shape[1]
    vmem, dma = pltpu.VMEM, pltpu.SemaphoreType.DMA
    any_ = pl.BlockSpec(memory_space=pltpu.HBM)
    inside = pl.BlockSpec(memory_space=pltpu.VMEM)
    return pl.pallas_call(
        comm_kernel,
        out_shape=(vmem((32, 16, ff), BF16), vmem((16, 32, d), BF16)),
        in_specs=[any_] * 4,
        out_specs=(inside, inside),
        scratch_shapes=[
            vmem((512, ff), BF16), vmem((ff, ff), BF16), vmem((4, 128, ff), F32),
            vmem((4, 128, ff), BF16), vmem((4, 128, ff), BF16),
            vmem((32, 16, ff), BF16), vmem((4, 2, 4, 16, ff), BF16),
            vmem((16, 32, d), BF16), vmem((d, d), BF16), vmem((16, 32, d), F32), vmem((16, 32, d), F32),
            dma((5,)), dma((1,)), dma((4, 8)), dma((1,)), dma((4,)), dma((1,)), dma((4, 2, 4)),
            dma((1,)), dma((4, 2, 4)), dma((1,)), dma((4,)),
            dma((1,)), dma((1,)), dma((1,)), dma((1,)), dma((1,)), dma((1,)), dma((1,)), dma((1,)),
        ],
        compiler_params=pltpu.CompilerParams(
            collective_id=0, has_side_effects=True, vmem_limit_bytes=60 << 20),
        name="gather_rotate",
    )(activations, out_grads, basis_in, basis_out)


TILES = ((0, 512), (512, 1024), (1024, 1536), (1536, 1848))


def diag_kernel(lens, rg, ra, out_hbm, out, masked, sem):
    starts, total = [], 0
    for s in range(8):
        starts.append(total)
        total = total + lens[s]
    longest, begin, most = 0, 0, lens[0]
    for s in range(1, 8):
        more = lens[s] > most
        longest = jnp.where(more, s, longest)
        begin = jnp.where(more, starts[s], begin)
        most = jnp.where(more, lens[s], most)
    token = lax.broadcasted_iota(jnp.int32, (256, 1), 0)
    wraps = token < begin
    low, high = ra[0:256, :], ra[256:512, :]
    masked[0] = jnp.where(wraps, high, low)
    others = jnp.where(wraps, low, high)
    for i in range(7):
        before = i < longest
        start = jnp.where(before, starts[i], starts[i + 1])
        length = jnp.where(before, lens[i], lens[i + 1])
        start = jnp.where(start >= 256, start - 256, start)
        keep = (token >= start) & (token < start + length)
        masked[i + 1] = jnp.where(keep, others, jnp.zeros_like(others))
    copies = []
    for index, (lo, hi) in enumerate(TILES):
        low, high = rg[0:256, lo:hi], rg[256:512, lo:hi]
        long_side = jnp.where(wraps, high, low).T
        other_side = jnp.where(wraps, low, high).T
        for i in range(8):
            p = jnp.dot(long_side if i == 0 else other_side, masked[i], preferred_element_type=F32)
            if i == 0:
                out[lo:hi, :] = p * p
            elif i < 7:
                out[lo:hi, :] += p * p
            else:
                out[lo:hi, :] = (out[lo:hi, :] + p * p) * (1.0 / 512.0)
        copies.append(pltpu.make_async_copy(
            out.at[pl.ds(lo, hi - lo)], out_hbm.at[pl.ds(lo, hi - lo)], sem.at[index]))
        copies[-1].start()
    for copy in copies:
        copy.wait()


def diagonal(lens, rg, ra):
    ff, d = rg.shape[1], ra.shape[1]
    inside = pl.BlockSpec(memory_space=pltpu.VMEM)
    return pl.pallas_call(
        diag_kernel,
        out_shape=jax.ShapeDtypeStruct((ff, d), F32),
        in_specs=[pl.BlockSpec(memory_space=pltpu.SMEM), inside, inside],
        out_specs=pl.BlockSpec(memory_space=pl.ANY),
        scratch_shapes=[
            pltpu.VMEM((ff, d), F32), pltpu.VMEM((8, 256, d), BF16), pltpu.SemaphoreType.DMA((4,))],
        compiler_params=pltpu.CompilerParams(vmem_limit_bytes=48 << 20),
        name="eigen_diagonal",
    )(lens, rg, ra)


def local(activations, out_grads, basis_in, basis_out, seq_lengths):
    rg, ra = gathered(activations, out_grads, basis_in, basis_out)
    rg = rg.reshape(512, rg.shape[-1])
    ra = ra.reshape(512, ra.shape[-1])
    return diagonal(seq_lengths, rg, ra)


def solution(mesh):
    in_specs = (P("row", "col"), P("col", "row"), P("col", "row"), P("row", "col"), P())
    out_specs = P("col", "row")
    return jax.shard_map(local, mesh=mesh, in_specs=in_specs, out_specs=out_specs, check_vma=False)
```

```python
import jax
import jax.numpy as jnp
from jax import lax
from jax.experimental import pallas as pl
from jax.experimental.pallas import tpu as pltpu
from jax.sharding import PartitionSpec as P

MESH = pl.DeviceIdType.MESH
F32, BF16 = jnp.float32, jnp.bfloat16
NZ, NY, NX = 8, 4, 4
PLUS, MINUS = 0, 1


def comm_kernel(act, grad, basis_in, basis_out, rg, ra,
                gbuf, bo, part, psend, sib, rsend, rrecv,
                abuf, bi, apart, arecv,
                lsem, g_send, g_recv, sib_send, sib_recv, rs_send, rs_recv,
                ag_send, ag_recv, agx_send, agx_recv,
                az_send, az_recv, ax_send, ax_recv, ar_send, ar_recv, aa_send, aa_recv):
    row, col = lax.axis_index("row"), lax.axis_index("col")
    z, k = row // 2, row % 2
    y, x = col // 4, col % 4

    def dev(z=z, k=k, y=y, x=x):
        return {"row": z * 2 + k, "col": y * 4 + x}

    def zrel(d):
        return (z + (d + NZ)) % NZ

    def xyrel(dy, dx):
        return (y + dy + NY) % NY, (x + dx + NX) % NX

    def remote(src, dst, ssem, rsem, to):
        pltpu.make_async_remote_copy(
            src_ref=src, dst_ref=dst, send_sem=ssem, recv_sem=rsem,
            device_id=to, device_id_type=MESH).start()

    def arrived(dst, ssem, rsem):
        pltpu.make_async_remote_copy(
            src_ref=dst, dst_ref=dst, send_sem=ssem, recv_sem=rsem,
            device_id=dev(), device_id_type=MESH).wait_recv()

    def sent(src, ssem, rsem):
        pltpu.make_async_remote_copy(
            src_ref=src, dst_ref=src, send_sem=ssem, recv_sem=rsem,
            device_id=dev(), device_id_type=MESH).wait_send()

    inner, outer = k == 0, k == 1

    loads = {}

    def load(name, src, dst):
        loads[name] = pltpu.make_async_copy(src, dst, lsem.at[len(loads)])
        loads[name].start()

    load("ga", grad.at[pl.ds(0, 16)], gbuf.at[pl.ds(0, 16)])
    load("gb", grad.at[pl.ds(16, 16)], gbuf.at[pl.ds(64, 16)])
    peers = [dev(z=zrel(d)) for d in range(1, NZ)]
    peers += [dev(k=1 - k)]
    for i in range(1, 16):
        py, px = xyrel(i // 4, i % 4)
        peers.append(dev(y=py, x=px))
    barrier = pltpu.get_barrier_semaphore()
    for peer in peers:
        pl.semaphore_signal(barrier, inc=1, device_id=peer, device_id_type=MESH)
    load("act", act, abuf.at[row])
    load("bo", basis_out, bo)
    load("bi", basis_in, bi)
    pl.semaphore_wait(barrier, len(peers))

    def gslot(e, j):
        if e in (1, 3):
            e, j = 1 if j % 4 < 2 else 3, j % 2 + (2 if e == 3 else 0) + (4 if j >= 4 else 0)
        return gbuf.at[pl.ds(128 * e + 16 * j, 16)]

    def gsend(src, e, j, to):
        remote(src, gslot(e, j), g_send.at[0], g_recv.at[e, 0 if e == 2 else j], to)

    def gsent():
        sent(gbuf.at[pl.ds(0, 480)], g_send.at[0], g_recv.at[0, 0])

    def last_arrived():
        arrived(gbuf.at[pl.ds(256, 128)], g_send.at[0], g_recv.at[2, 0])

    def garrived(e, j):
        arrived(gslot(e, j), g_send.at[0], g_recv.at[e, j])

    def xy(dy, dx):
        py, px = xyrel(dy, dx)
        return dev(y=py, x=px)

    loads["ga"].wait()
    loads["gb"].wait()
    for d in (1, 3, 2):
        gsend(gslot(0, 0), 0, d, xy(0, -d))
        gsend(gslot(0, 4), 0, 4 + d, xy(-d, 0))
    gsend(gslot(0, 0), 1, 0, xy(-1, 0))
    gsend(gslot(0, 0), 3, 0, xy(1, 0))
    gsend(gslot(0, 4), 1, 4, xy(0, -1))
    gsend(gslot(0, 4), 3, 4, xy(0, 1))

    loads["act"].wait()
    for i, d in enumerate((1, 7, 2, 6, 3, 5, 4)):
        remote(abuf.at[row], abuf.at[row], az_send.at[0], az_recv.at[0], dev(z=zrel(-d)))
    remote(abuf.at[row], abuf.at[row], ax_send.at[0], ax_recv.at[0], dev(k=1 - k))

    for d in (1, 3, 2):
        garrived(0, d)
        gsend(gslot(0, d), 1, d, xy(-1, 0))
        gsend(gslot(0, d), 3, d, xy(1, 0))
        garrived(0, 4 + d)
        gsend(gslot(0, 4 + d), 1, 4 + d, xy(0, -1))
        gsend(gslot(0, 4 + d), 3, 4 + d, xy(0, 1))

    def far(e, j):
        garrived(e, j)
        step = -1 if e == 1 else 1
        gsend(gslot(e, j), 2, j, xy(step, 0) if j < 4 else xy(0, step))

    far(1, 0)
    far(1, 4)

    sibling = dev(k=1 - k)

    def product(e):
        for lo, hi in ((0, 512), (512, 1024), (1024, 1536), (1536, 1848)):
            value = jnp.dot(gbuf[128 * e:128 * e + 128], bo[:, lo:hi], preferred_element_type=F32)

            @pl.when(inner)
            def _():
                psend[e, :, lo:hi] = value.astype(BF16)

            @pl.when(outer)
            def _():
                part[e, :, lo:hi] = value

        @pl.when(inner)
        def _():
            remote(psend.at[e], sib.at[e], sib_send.at[0], sib_recv.at[e], sibling)

    def own(e, j):
        at = pl.ds(pl.multiple_of(16 * j, 16), 16)
        return part[e, at, :] + sib[e, at, :].astype(F32)

    def long_way(e):
        return PLUS if e < 2 else MINUS

    def rs_send_own(e, way, index, to_owner, to):
        sign = 1 if way == PLUS else -1
        rsend[8 * e + 4 * way + index] = own(e, zrel(sign * to_owner)).astype(BF16)
        remote(rsend.at[8 * e + 4 * way + index], rrecv.at[e, way, index],
               rs_send.at[0], rs_recv.at[e, way, index], dev(z=zrel(sign * to)))

    def rs_take(e, way, index):
        arrived(rrecv.at[e, way, index], rs_send.at[0], rs_recv.at[e, way, index])
        return rrecv[e, way, index].astype(F32)

    def rs_start(e):
        rs_send_own(e, long_way(e), 1, 4, 2)
        for way in (long_way(e), 1 - long_way(e)):
            rs_send_own(e, way, 0, 3, 1)
        for way in (long_way(e), 1 - long_way(e)):
            rs_send_own(e, way, 2, 1, 1)

    def rs_relay(e, way):
        sign = 1 if way == PLUS else -1
        value = own(e, zrel(sign * 2)) + rs_take(e, way, 0)
        if way == long_way(e):
            value = value + rs_take(e, way, 1)
        rsend[8 * e + 4 * way + 3] = value.astype(BF16)
        remote(rsend.at[8 * e + 4 * way + 3], rrecv.at[e, way, 3],
               rs_send.at[0], rs_recv.at[e, way, 3], dev(z=zrel(sign * 2)))

    def block_of(e, j):
        if e in (1, 3):
            other, away = j % 2 + (e - 1), jnp.where((j // 2) % 2 == 0, 1, 3)
        else:
            other, away = j % 4, e
        first = 2 * (((y + away) % 4) * 4 + (x + other) % 4)
        second = 2 * (((y + other) % 4) * 4 + (x + away) % 4) + 1
        return jnp.where(j < 4, first, second)

    def rs_end(e):
        value = own(e, z)
        for index in (2, 3):
            for way in (PLUS, MINUS):
                value = value + rs_take(e, way, index)
        rg[block_of(e, z)] = value.astype(BF16)

    def over(e, d):
        at = rg.at[block_of(e, zrel(d))]
        remote(at, at, agx_send.at[0], agx_recv.at[e], sibling)

    def ag_hop(e, way, hop):
        sign = 1 if way == PLUS else -1
        last = 4 if way == long_way(e) else 3
        if hop > last:
            return
        at = rg.at[block_of(e, zrel(-sign * hop))]
        if hop > 0:
            arrived(at, ag_send.at[0], ag_recv.at[e, way, hop - 1])
        if hop < last:
            remote(at, at, ag_send.at[0], ag_recv.at[e, way, hop], dev(z=zrel(sign)))

    def ag_send_block(e, way, index, d, to):
        sign = 1 if way == PLUS else -1
        at = rg.at[block_of(e, zrel(d))]
        remote(at, at, ag_send.at[0], ag_recv.at[e, way, index], dev(z=zrel(sign * to)))

    def ag_take(e, way, index, d):
        at = rg.at[block_of(e, zrel(d))]
        arrived(at, ag_send.at[0], ag_recv.at[e, way, index])

    def start(e):
        arrived(sib.at[e], sib_send.at[0], sib_recv.at[e])
        rs_start(e)

    def end(e):
        rs_end(e)
        ways = (long_way(e), 1 - long_way(e))
        if e in (0, 1):
            for way in ways:
                ag_hop(e, way, 0)
        else:
            for index in (1, 0):
                for way in ways:
                    ag_send_block(e, way, index, 0, index + 1)
        over(e, 0)

    def hop(e, way, n):
        ag_hop(e, way, n)
        over(e, (-1 if way == PLUS else 1) * n)

    def forward(e, way):
        sign = 1 if way == PLUS else -1
        ag_take(e, way, 1, -2 * sign)
        if way == long_way(e):
            ag_send_block(e, way, 3, -2 * sign, 2)
        ag_send_block(e, way, 2, -2 * sign, 1)
        over(e, -2 * sign)

    def take(e, way, n):
        sign = 1 if way == PLUS else -1
        ag_take(e, way, {1: 0, 3: 2, 4: 3}[n], -n * sign)
        over(e, -n * sign)

    def steps(*todo):
        @pl.when(outer)
        def _():
            for act, *what in todo:
                act(*what)

    def acts_over():
        arrived(abuf.at[pl.ds(0, 7)], az_send.at[0], az_recv.at[0])
        for d in range(1, NZ):
            r = zrel(d) * 2 + k
            remote(abuf.at[r], abuf.at[r], ax_send.at[0], ax_recv.at[0], sibling)

    def acts_product():
        loads["bi"].wait()
        arrived(abuf.at[pl.ds(0, 8)], ax_send.at[0], ax_recv.at[0])
        for lo in range(0, 16, 4):
            value = jnp.dot(abuf[lo:lo + 4].reshape(128, 512), bi[...], preferred_element_type=F32)
            apart[lo:lo + 4] = value.reshape(4, 32, 512)
        for i in range(1, 16):
            py, px = xyrel(-(i // 4), -(i % 4))
            remote(apart.at[py * 4 + px], arecv.at[i], ar_send.at[0], ar_recv.at[0], dev(y=py, x=px))

    def acts_sum():
        value = apart[col]
        arrived(arecv.at[pl.ds(1, 15)], ar_send.at[0], ar_recv.at[0])
        for i in range(1, 16):
            value = value + arecv[i]
        ra[col] = value.astype(BF16)
        for i in range(1, 16):
            py, px = xyrel(-(i // 4), -(i % 4))
            remote(ra.at[col], ra.at[col], aa_send.at[0], aa_recv.at[0], dev(y=py, x=px))

    def acts_end():
        arrived(ra.at[pl.ds(0, 15)], aa_send.at[0], aa_recv.at[0])

    loads["bo"].wait()
    product(0)
    for j in (1, 5):
        far(1, j)
    for j in (3, 7):
        far(3, j)
    for j in (0, 1, 4, 5):
        garrived(3, j)
    product(1)
    for j in (2, 6):
        far(3, j)
    steps(
        (start, 0),
    )
    for j in (2, 3, 6, 7):
        garrived(1, j)
    product(3)
    acts_over()
    steps(
        (start, 1),
    )
    last_arrived()
    product(2)
    steps(
        (start, 3),
        (rs_relay, 0, MINUS),
        (rs_relay, 0, PLUS),
        (rs_relay, 1, MINUS),
        (start, 2),
        (rs_relay, 1, PLUS),
        (rs_relay, 3, PLUS),
        (rs_relay, 3, MINUS),
        (rs_relay, 2, PLUS),
    )
    acts_product()
    steps(
        (end, 0),
        (end, 1),
        (rs_relay, 2, MINUS),
        (hop, 0, PLUS, 1),
        (end, 3),
        (hop, 1, PLUS, 1),
        (hop, 0, MINUS, 1),
        (hop, 1, MINUS, 1),
        (end, 2),
        (hop, 0, PLUS, 2),
        (forward, 3, MINUS),
    )
    acts_sum()
    steps(
        (forward, 3, PLUS),
        (take, 3, MINUS, 1),
        (take, 3, PLUS, 1),
        (hop, 0, MINUS, 2),
        (hop, 1, PLUS, 2),
        (hop, 1, MINUS, 2),
        (forward, 2, PLUS),
        (take, 2, PLUS, 1),
        (forward, 2, MINUS),
        (take, 2, MINUS, 1),
        (hop, 0, PLUS, 3),
        (take, 3, PLUS, 3),
        (hop, 1, PLUS, 3),
        (take, 3, MINUS, 4),
        (take, 3, MINUS, 3),
        (take, 2, PLUS, 3),
        (hop, 0, MINUS, 3),
        (hop, 0, PLUS, 4),
        (hop, 1, MINUS, 3),
        (hop, 1, PLUS, 4),
        (take, 2, MINUS, 4),
        (take, 2, MINUS, 3),
    )
    acts_end()

    gsent()
    sent(abuf.at[pl.ds(0, 7)], az_send.at[0], az_recv.at[0])
    sent(abuf.at[pl.ds(0, 8)], ax_send.at[0], ax_recv.at[0])
    sent(apart.at[pl.ds(0, 15)], ar_send.at[0], ar_recv.at[0])
    sent(ra.at[pl.ds(0, 15)], aa_send.at[0], aa_recv.at[0])

    @pl.when(inner)
    def _():
        sent(psend, sib_send.at[0], sib_recv.at[0])
        for e in (0, 1, 3, 2):
            arrived(rg.at[pl.ds(8 * e, 8)], agx_send.at[0], agx_recv.at[e])

    @pl.when(outer)
    def _():
        sent(rsend.at[pl.ds(0, 28)], rs_send.at[0], rs_recv.at[0, 0, 0])
        sent(rg.at[pl.ds(0, 28)], ag_send.at[0], ag_recv.at[0, 0, 0])
        sent(rg, agx_send.at[0], agx_recv.at[0])


def gathered(activations, out_grads, basis_in, basis_out):
    ff, d = basis_out.shape[1], basis_in.shape[1]
    vmem, dma = pltpu.VMEM, pltpu.SemaphoreType.DMA
    any_ = pl.BlockSpec(memory_space=pltpu.HBM)
    inside = pl.BlockSpec(memory_space=pltpu.VMEM)
    return pl.pallas_call(
        comm_kernel,
        out_shape=(vmem((32, 16, ff), BF16), vmem((16, 32, d), BF16)),
        in_specs=[any_] * 4,
        out_specs=(inside, inside),
        scratch_shapes=[
            vmem((512, ff), BF16), vmem((ff, ff), BF16), vmem((4, 128, ff), F32),
            vmem((4, 128, ff), BF16), vmem((4, 128, ff), BF16),
            vmem((32, 16, ff), BF16), vmem((4, 2, 4, 16, ff), BF16),
            vmem((16, 32, d), BF16), vmem((d, d), BF16), vmem((16, 32, d), F32), vmem((16, 32, d), F32),
            dma((5,)), dma((1,)), dma((4, 8)), dma((1,)), dma((4,)), dma((1,)), dma((4, 2, 4)),
            dma((1,)), dma((4, 2, 4)), dma((1,)), dma((4,)),
            dma((1,)), dma((1,)), dma((1,)), dma((1,)), dma((1,)), dma((1,)), dma((1,)), dma((1,)),
        ],
        compiler_params=pltpu.CompilerParams(
            collective_id=0, has_side_effects=True, vmem_limit_bytes=60 << 20),
        name="gather_rotate",
    )(activations, out_grads, basis_in, basis_out)


TILES = ((0, 512), (512, 1024), (1024, 1536), (1536, 1848))


def diag_kernel(lens, rg, ra, out_hbm, out, masked, sem):
    starts, total = [], 0
    for s in range(8):
        starts.append(total)
        total = total + lens[s]
    longest, begin, most = 0, 0, lens[0]
    for s in range(1, 8):
        more = lens[s] > most
        longest = jnp.where(more, s, longest)
        begin = jnp.where(more, starts[s], begin)
        most = jnp.where(more, lens[s], most)
    token = lax.broadcasted_iota(jnp.int32, (256, 1), 0)
    wraps = token < begin
    low, high = ra[0:256, :], ra[256:512, :]
    masked[0] = jnp.where(wraps, high, low)
    others = jnp.where(wraps, low, high)
    for i in range(7):
        before = i < longest
        start = jnp.where(before, starts[i], starts[i + 1])
        length = jnp.where(before, lens[i], lens[i + 1])
        start = jnp.where(start >= 256, start - 256, start)
        keep = (token >= start) & (token < start + length)
        masked[i + 1] = jnp.where(keep, others, jnp.zeros_like(others))
    copies = []
    for index, (lo, hi) in enumerate(TILES):
        low, high = rg[0:256, lo:hi], rg[256:512, lo:hi]
        long_side = jnp.where(wraps, high, low).T
        other_side = jnp.where(wraps, low, high).T
        for i in range(8):
            p = jnp.dot(long_side if i == 0 else other_side, masked[i], preferred_element_type=F32)
            if i == 0:
                out[lo:hi, :] = p * p
            elif i < 7:
                out[lo:hi, :] += p * p
            else:
                out[lo:hi, :] = (out[lo:hi, :] + p * p) * (1.0 / 512.0)
        copies.append(pltpu.make_async_copy(
            out.at[pl.ds(lo, hi - lo)], out_hbm.at[pl.ds(lo, hi - lo)], sem.at[index]))
        copies[-1].start()
    for copy in copies:
        copy.wait()


def diagonal(lens, rg, ra):
    ff, d = rg.shape[1], ra.shape[1]
    inside = pl.BlockSpec(memory_space=pltpu.VMEM)
    return pl.pallas_call(
        diag_kernel,
        out_shape=jax.ShapeDtypeStruct((ff, d), F32),
        in_specs=[pl.BlockSpec(memory_space=pltpu.SMEM), inside, inside],
        out_specs=pl.BlockSpec(memory_space=pl.ANY),
        scratch_shapes=[
            pltpu.VMEM((ff, d), F32), pltpu.VMEM((8, 256, d), BF16), pltpu.SemaphoreType.DMA((4,))],
        compiler_params=pltpu.CompilerParams(vmem_limit_bytes=48 << 20),
        name="eigen_diagonal",
    )(lens, rg, ra)


def local(activations, out_grads, basis_in, basis_out, seq_lengths):
    rg, ra = gathered(activations, out_grads, basis_in, basis_out)
    rg = rg.reshape(512, rg.shape[-1])
    ra = ra.reshape(512, ra.shape[-1])
    return diagonal(seq_lengths, rg, ra)


def solution(mesh):
    in_specs = (P("row", "col"), P("col", "row"), P("col", "row"), P("row", "col"), P())
    out_specs = P("col", "row")
    return jax.shard_map(local, mesh=mesh, in_specs=in_specs, out_specs=out_specs, check_vma=False)
```
